512 devices in a mesh: region: 64 (over z, x), member: 8 (over y, core).
Axes of the slice: x: 4, y: 4, z: 16, core: 2. Of those that a mesh axis runs over, the one named last changes fastest.
Arguments:
- perturbations: bfloat16 [80, 2, 64, 8192], P('member', None, None, 'region'), may hold values from -0.65625 to 0.65625
- control: float32 [80, 64, 8192], P('member', None, 'region'), may hold values from -6 to 6
- vertical_loc: bfloat16 [64, 64], replicated, may hold values from -0.75 to 0.75
- block_kernels: bfloat16 [4, 128, 128], replicated, may hold values from -0.3125 to 0.3125
- loc_pattern: int32 [64, 3], replicated, may hold values from 0 to 3
- obs_region: int32 [65536, 1], P('region'), may hold values from 0 to 63; in each aligned block of 128 rows (0 to 127, 128 to 255, ...) at most 4 rows name the same one
- obs_slot: int32 [65536], P('region'), may hold values from 0 to 1
- obs_cell: int32 [65536], P('region'), may hold values from 0 to 127
- innovations: float32 [64, 65536], P(None, 'region'), may hold values from -12 to 12
- obs_weight: float32 [512, 128, 128], P('region'), may hold values from -0.0375 to 2, as said below
Outputs:
- analysis: float32 [80, 64, 8192], P('member', None, 'region')
The draws below stay inside these ranges and needn't reach their ends.
Inputs may be any that keep to these rules, and one draw needn't show every extreme that they name: `obs_region`: in each aligned block of 128 rows, no region is named by more than 4 rows. `obs_weight`: each tile is symmetric, and in each row the diagonal entry exceeds the sum of the magnitudes of the other entries.
All inputs are finite; a program needn't handle non-finite values.
Results may differ from the reference program's by a relative error of at most 0.013.
Values may be sent and summed in bfloat16 or wider, within the bound.
A program may use at most 64 MiB of HBM per device.

```python
import math
import jax
import jax.numpy as jnp
import numpy as np
from jax import lax

LEV = 64
MEMBERS = 80
SLOTS = 2
BLOCK = 128
TILE = 128
KTYPES = 4
ITERS = 2
CELLS_DEV = 128
OBS_DEV = 1024
REGIONS = 64
NCELLS = 8192
NBLOCKS = 64
OBS = 65536
TILES = 512
OBS_GROUP = 128
CAP = 4


def draw_innovations(key, part):
    columns = jnp.arange(OBS, dtype=jnp.int32)
    region_share = (columns // OBS_DEV).astype(jnp.float32) / max(REGIONS - 1, 1)
    scaling = 1.0 + 2.0 * region_share
    values = jnp.clip(jax.random.normal(key, (LEV, OBS), jnp.float32), -4.0, 4.0)
    return values * scaling[None, :]


def draw_obs_weight(key, part):
    key_diag = jax.random.fold_in(key, 11)
    key_off = jax.random.fold_in(key, 13)
    diagonal = jax.random.uniform(key_diag, (TILES, TILE), jnp.float32, 1.0, 2.0)
    raw_values = jax.random.uniform(key_off, (TILES, TILE, TILE), jnp.float32, -1.0, 1.0)
    mixed = 0.5 * (raw_values + jnp.swapaxes(raw_values, 1, 2))
    indices = jnp.arange(TILE, dtype=jnp.int32)
    spacing = jnp.abs(indices[:, None] - indices[None, :]).astype(jnp.float32)
    falloff = jnp.where(spacing > 0.0, jnp.exp(-spacing / 8.0), 0.0)
    identity = jnp.where(spacing > 0.0, 0.0, 1.0)
    return diagonal[:, :, None] * identity[None] + 0.0375 * mixed * falloff[None]


def touch_ends(drawn, rng, least, high):
    longest = drawn.shape.index(max(drawn.shape))
    spots = []
    for shift in (0, 1):
        where = [jax.random.randint(jax.random.fold_in(rng, axis), (), 0, length) for axis, length in enumerate(drawn.shape)]
        where[longest] = (where[longest] + shift) % drawn.shape[longest]
        spots.append(tuple(where))
    return drawn.at[spots[0]].set(least).at[spots[1]].set(high)


def steps_of(stream_key, shape, split, smallest, largest):
    def one(dim, parts):
        steps = jax.random.uniform(jax.random.fold_in(jax.random.fold_in(stream_key, 6), dim), (parts,), jnp.float32, smallest / len(split), largest / len(split))
        return jnp.repeat(jnp.exp(steps), shape[dim] // parts).reshape((-1,) + (1,) * (len(shape) - dim - 1))

    gain = one(*split[0])
    for cut in split[1:]:
        gain = gain * one(*cut)
    return gain


def assign_block(key, own, number, rows, count, top, most, slope):
    order = jax.random.permutation(key, count)
    packed, usual = shares(count, rows * top, most, slope, True), shares(count, rows * top, most, slope, False)
    places = jnp.arange(count)

    def named(lengths, rotation):
        used = int((lengths > 0).sum())
        fixed = max(1, used // 4)
        shifted = fixed + (places - fixed + rotation * (used - fixed)) % max(1, count - fixed)
        return jnp.zeros((count,), jnp.int32).at[order[jnp.where(places < fixed, places, shifted)]].set(jnp.asarray(lengths, jnp.int32))

    lengths = jnp.where(number % 4 == 0, named(packed, number // 4), named(usual, number - number // 4 - 1))
    mixed = jax.random.permutation(jax.random.fold_in(own, 3), count)
    donor, sink = mixed[0:count // 2 * 2:2], mixed[1:count // 2 * 2:2]
    room = jnp.minimum(lengths[donor] - 1, most - lengths[sink]) // 2
    room = jnp.where((donor == order[0]) | (sink == order[0]) | (lengths[sink] == 0), 0, jnp.maximum(room, 0))
    shifted = jax.random.randint(jax.random.fold_in(own, 4), (count // 2,), 0, 1 << 20) % (room + 1)
    lengths = lengths.at[donor].add(-shifted).at[sink].add(shifted)
    items = jnp.searchsorted(jnp.cumsum(lengths), jnp.arange(rows * top), side="right").astype(jnp.int32)
    listing = items.reshape(top, rows).T
    listing = listing[jax.random.permutation(jax.random.fold_in(own, 1), rows)]
    rotation = jax.random.randint(jax.random.fold_in(own, 2), (rows, 1), 0, top)
    return jnp.take_along_axis(listing, (jnp.arange(top)[None, :] + rotation) % top, axis=1)


def shares(count, total, most, slope, full):
    loads = [(1 << 20) // math.isqrt(standing ** slope) + 1 for standing in range(1, count + 1)]
    largest = most if full else min(most, max(-(-total // count), total * loads[0] // sum(loads)))
    least = 1 if total - largest >= count - 1 else 0
    given, spare = [largest] + [least] * (count - 1), total - largest - least * (count - 1)
    while spare > 0:
        free = [i for i in range(1, count) if given[i] < largest] or [i for i in range(1, count) if given[i] < most]
        whole, left = sum([loads[i] for i in free]), spare
        for i in free:
            extra = min(most - given[i], max(1, left * loads[i] // whole), spare)
            given[i] = given[i] + extra
            spare = spare - extra
    return np.array(given)


def scatter_about(rng, shape, scale, bound, cuts=(), held_as=jnp.bfloat16):
    loudness = steps_of(rng, shape, cuts, -0.22, 0.18) if cuts else 1.0
    array = jax.random.normal(rng, shape, jnp.float32) * scale * loudness
    return jnp.minimum(jnp.maximum(array, -bound), bound).astype(held_as)


def setup_inputs(seed: int = 0) -> dict:
    splits = jax.random.split(jax.random.key(seed), 11)
    perturbations = scatter_about(splits[0], (MEMBERS, SLOTS, LEV, NCELLS), 0.11, 0.65625, ((0, 8), (3, 64)))
    control = scatter_about(splits[1], (MEMBERS, LEV, NCELLS), 1.0, 6.0, ((0, 8), (2, 64)), jnp.float32)
    vertical_loc = scatter_about(splits[2], (LEV, LEV), LEV ** -0.5, 0.75)
    block_kernels = scatter_about(splits[3], (KTYPES, BLOCK, BLOCK), (3 * BLOCK) ** -0.5, 0.3125)
    loc_pattern = touch_ends(jax.random.randint(splits[4], (NBLOCKS, 3), 0, KTYPES), jax.random.fold_in(splits[4], 1), 0, KTYPES - 1).astype(jnp.int32)
    obs_region_keys = jax.random.split(jax.random.fold_in(splits[5], 1), OBS // OBS_GROUP)
    obs_region_turns = jax.random.permutation(jax.random.fold_in(splits[5], 3), OBS // OBS_GROUP)
    obs_region = jax.vmap(lambda own, number: assign_block(jax.random.fold_in(splits[5], 2), own, number, OBS_GROUP, REGIONS, 1, CAP, 2))(obs_region_keys, obs_region_turns).reshape((OBS, 1))
    obs_slot = touch_ends(jax.random.randint(splits[6], (OBS,), 0, SLOTS), jax.random.fold_in(splits[6], 1), 0, SLOTS - 1).astype(jnp.int32)
    obs_cell = touch_ends(jax.random.randint(splits[7], (OBS,), 0, CELLS_DEV), jax.random.fold_in(splits[7], 1), 0, CELLS_DEV - 1).astype(jnp.int32)
    innovations = draw_innovations(jax.random.fold_in(splits[10], 71), 0)
    obs_weight = draw_obs_weight(jax.random.fold_in(splits[10], 71), 0)
    return {"perturbations": perturbations, "control": control, "vertical_loc": vertical_loc, "block_kernels": block_kernels, "loc_pattern": loc_pattern, "obs_region": obs_region, "obs_slot": obs_slot, "obs_cell": obs_cell, "innovations": innovations, "obs_weight": obs_weight}


def horizontal(values, tables):
    padded = jnp.pad(values, ((0, 0), (BLOCK, BLOCK)))
    summed = jnp.zeros((LEV, NBLOCKS, BLOCK), jnp.float32)
    for offset in range(3):
        window = padded[:, offset * BLOCK: offset * BLOCK + NCELLS].reshape(LEV, NBLOCKS, BLOCK)
        summed = summed + jnp.einsum("lbk,bkj->lbj", window.astype(jnp.float32), tables[offset])
    return summed.reshape(LEV, NCELLS)


def horizontal_adjoint(values, tables):
    padded = jnp.pad(values, ((0, 0), (BLOCK, BLOCK)))
    summed = jnp.zeros((LEV, NBLOCKS, BLOCK), jnp.float32)
    for offset in range(3):
        first_cell = (2 - offset) * BLOCK
        window = padded[:, first_cell: first_cell + NCELLS].reshape(LEV, NBLOCKS, BLOCK)
        summed = summed + jnp.einsum("lbj,bkj->lbk", window.astype(jnp.float32), tables[offset])
    return summed.reshape(LEV, NCELLS)


def reference(perturbations, control, vertical_loc, block_kernels, loc_pattern, obs_region, obs_slot, obs_cell, innovations, obs_weight):
    pattern_pad = jnp.pad(loc_pattern, ((1, 1), (0, 0)))
    forward_tables = [block_kernels[loc_pattern[:, offset]].astype(jnp.float32) for offset in range(3)]
    backward_tables = [block_kernels[pattern_pad[2 - offset: 2 - offset + NBLOCKS, offset]].astype(jnp.float32) for offset in range(3)]
    obs_codes = (obs_slot * NCELLS + obs_region[:, 0] * CELLS_DEV + obs_cell).astype(jnp.int32)

    def apply_operator(vector, with_innovation):
        def forward_member(running, inputs):
            member_vector, member_pert = inputs
            spread = horizontal(member_vector.astype(jnp.bfloat16), forward_tables).astype(jnp.bfloat16)
            weights = jnp.dot(vertical_loc, spread, preferred_element_type=jnp.float32)
            return running + member_pert.astype(jnp.float32) * weights[None], None

        increment, _ = lax.scan(forward_member, jnp.zeros((SLOTS, LEV, NCELLS), jnp.float32), (vector, perturbations))
        flattened = increment.transpose(1, 0, 2).reshape(LEV, SLOTS * NCELLS)
        departures = flattened[:, obs_codes]
        if with_innovation:
            departures = departures - innovations
        weighted = jnp.einsum("ltk,tkj->ltj", departures.reshape(LEV, TILES, TILE), obs_weight,
                              precision=lax.Precision.HIGHEST).reshape(LEV, OBS)
        adjoint_flat = jnp.zeros((LEV, SLOTS * NCELLS), jnp.float32).at[:, obs_codes].add(weighted)
        adjoint_field = adjoint_flat.reshape(LEV, SLOTS, NCELLS).transpose(1, 0, 2)

        def backward_member(inputs):
            member_vector, member_pert = inputs
            projected = jnp.sum(member_pert.astype(jnp.float32) * adjoint_field, axis=0).astype(jnp.bfloat16)
            lifted = jnp.dot(vertical_loc.T, projected, preferred_element_type=jnp.float32).astype(jnp.bfloat16)
            return member_vector + horizontal_adjoint(lifted, backward_tables)

        return lax.map(backward_member, (vector, perturbations))

    residual = -apply_operator(control, True)
    direction = residual
    norm_now = jnp.sum(residual * residual)
    solution = control
    for iteration in range(ITERS):
        curved = apply_operator(direction, False)
        step_size = norm_now / jnp.sum(direction * curved)
        solution = solution + step_size * direction
        if iteration + 1 < ITERS:
            residual = residual - step_size * curved
            norm_next = jnp.sum(residual * residual)
            direction = residual + (norm_next / norm_now) * direction
            norm_now = norm_next
    return solution
```

```python
import jax
import jax.numpy as jnp
from jax import lax
from jax.experimental import pallas as pl
from jax.experimental.pallas import tpu as pltpu
from jax.sharding import PartitionSpec as P

REGIONS, MEMBERS = 64, 8
OWN = 10
LEV, CELLS = 64, 128
ROWS = OWN * LEV
TILES = 8
LPM = LEV // MEMBERS
KTYPES = 4
F32, BF16 = jnp.float32, jnp.bfloat16
MESH = pl.DeviceIdType.MESH
CODES, SAMPLES, RETURNS, SCALARS = 0, (1, 3, 5), (2, 4), 6
SUMS, ADJOINTS, MEMBER_SCALARS = (0, 2, 4), (1, 3), 5
VECTORS, LIFTED = (0, 2, 4), (1, 3)


def dot(a, b):
    return jnp.dot(a, b, preferred_element_type=F32)


def dot_nt(a, b):
    return lax.dot_general(a, b, (((1,), (1,)), ((), ())), preferred_element_type=F32)


def bit_of(shape, axis, stride):
    return (lax.broadcasted_iota(jnp.int32, shape, axis) & stride) != 0


def swap_bits(x, row_stride, lane_stride):
    n = x.shape[0]
    row, lane = bit_of(x.shape, 0, row_stride), bit_of(x.shape, 1, lane_stride)
    up = pltpu.roll(pltpu.roll(x, n - row_stride, 0), lane_stride, 1)
    down = pltpu.roll(pltpu.roll(x, row_stride, 0), CELLS - lane_stride, 1)
    return jnp.where(row == lane, x, jnp.where(row, down, up))


def region_major(x):
    return swap_bits(swap_bits(x, 2, 32), 4, 64)


def tile_major(x):
    return swap_bits(swap_bits(swap_bits(x, 8, 4), 16, 8), 32, 16)


def split(x):
    high = x.astype(BF16)
    return high, (x - high.astype(F32)).astype(BF16)


def kernel(
    pert_ref, control_ref, vloc_ref, table_ref, pattern_ref, region_ref, code_ref, innov_ref, weight_ref,
    out_ref,
    pert, weight, innov, r0, q, halo_out, halo_in, own_lift,
    cols_out, cols_in, part_out, part_in,
    onehot, coupling, innov_slots, blocks, vert,
    load_sem, bar_done, col_send, col_recv, part_send, part_recv, halo_send, halo_recv,
):
    region, member = lax.axis_index("region"), lax.axis_index("member")
    left, right = lax.rem(region + (REGIONS - 1), REGIONS), lax.rem(region + 1, REGIONS)

    loads = [
        pltpu.make_async_copy(pert_ref, pert, load_sem.at[0]),
        pltpu.make_async_copy(weight_ref, weight, load_sem.at[1]),
        pltpu.make_async_copy(innov_ref.at[pl.ds(pl.multiple_of(member * LPM, LPM), LPM)], innov, load_sem.at[2]),
    ]
    barrier = pltpu.get_barrier_semaphore()

    def greet_region(i, _):
        pl.semaphore_signal(
            barrier, inc=1, device_id={"region": lax.rem(region + i, REGIONS)}, device_id_type=MESH
        )
        return 0

    lax.fori_loop(1, REGIONS, greet_region, 0)

    def greet_member(i, _):
        pl.semaphore_signal(
            barrier, inc=1, device_id={"member": lax.rem(member + i, MEMBERS)}, device_id_type=MESH
        )
        return 0

    lax.fori_loop(1, MEMBERS, greet_member, 0)
    for load in (loads[1], loads[2], loads[0]):
        load.start()

    def start_columns(n):
        def one(i):
            to = lax.rem(region + i, REGIONS)
            pltpu.make_async_remote_copy(
                src_ref=cols_out.at[n, to], dst_ref=cols_in.at[n, region],
                send_sem=col_send.at[n], recv_sem=col_recv.at[n],
                device_id={"region": to}, device_id_type=MESH,
            ).start()

        def pair(j, _):
            one(32 - j)
            one(32 + j)
            return 0

        one(32)
        lax.fori_loop(1, 32, pair, 0)

    def columns_like(n):
        return pltpu.make_async_remote_copy(
            src_ref=cols_out.at[n, pl.ds(0, REGIONS - 1)], dst_ref=cols_in.at[n, pl.ds(0, REGIONS - 1)],
            send_sem=col_send.at[n], recv_sem=col_recv.at[n],
            device_id={"region": right}, device_id_type=MESH,
        )

    def start_parts(n, same):
        def one(i, _):
            to = lax.rem(member + i, MEMBERS)
            pltpu.make_async_remote_copy(
                src_ref=part_out.at[n, member if same else to], dst_ref=part_in.at[n, member],
                send_sem=part_send.at[n], recv_sem=part_recv.at[n],
                device_id={"member": to}, device_id_type=MESH,
            ).start()
            return 0

        lax.fori_loop(1, MEMBERS, one, 0)

    def parts_like(n):
        return pltpu.make_async_remote_copy(
            src_ref=part_out.at[n, pl.ds(0, MEMBERS - 1)], dst_ref=part_in.at[n, pl.ds(0, MEMBERS - 1)],
            send_sem=part_send.at[n], recv_sem=part_recv.at[n],
            device_id={"member": lax.rem(member + 1, MEMBERS)}, device_id_type=MESH,
        )

    def halo(n, side):
        return pltpu.make_async_remote_copy(
            src_ref=halo_out.at[n], dst_ref=halo_in.at[n, 1 - side],
            send_sem=halo_send.at[n, side], recv_sem=halo_recv.at[n, 1 - side],
            device_id={"region": left if side == 0 else right}, device_id_type=MESH,
        )

    def wait_halo(n, side):
        pltpu.make_async_remote_copy(
            src_ref=halo_out.at[n], dst_ref=halo_in.at[n, side],
            send_sem=halo_send.at[n, 1 - side], recv_sem=halo_recv.at[n, side],
            device_id={"region": left if side == 0 else right}, device_id_type=MESH,
        ).wait_recv()

    def send_columns(n, x):
        cols_out[n] = region_major(x).reshape(REGIONS, 2, CELLS)
        cols_in[n, region] = cols_out[n, region]
        start_columns(n)

    def get_columns(n):
        columns_like(n).wait_recv()
        return region_major(cols_in[n].reshape(2 * REGIONS, CELLS))

    halo_out[VECTORS[0]] = control_ref[...].astype(BF16)

    regions8 = region_ref[...]
    codes8 = code_ref[...].astype(F32).astype(BF16)
    iota_row = lax.broadcasted_iota(jnp.int32, (CELLS, CELLS), 0)
    iota_lane = lax.broadcasted_iota(jnp.int32, (CELLS, CELLS), 1)
    identity = (iota_row == iota_lane).astype(F32).astype(BF16)
    zz, xx = regions8 >> 2, regions8 & 3
    base8 = 128 * (zz >> 3) + 32 * xx + 4 * (zz & 7)
    base_cols = dot_nt(identity, base8.astype(F32).astype(BF16)).astype(jnp.int32)
    slot_lane = lax.broadcasted_iota(jnp.int32, (CELLS, 2 * CELLS), 1)
    slot_row = lax.broadcasted_iota(jnp.int32, (2 * CELLS, CELLS), 0)
    tile_rows = lax.broadcasted_iota(jnp.int32, (8, 2 * CELLS), 0)
    code_halves = [[], []]
    placing, placing_t = [], []
    for t in range(TILES):
        col, row = base_cols[:, t : t + 1], base8[t : t + 1, :]
        same = col == row
        rank_col = jnp.sum((same & (iota_lane < iota_row)).astype(F32), axis=1, keepdims=True)
        rank_row = jnp.sum((same & (iota_row < iota_lane)).astype(F32), axis=0, keepdims=True)
        place = (slot_lane == col + rank_col.astype(jnp.int32)).astype(F32).astype(BF16)
        place_t = (slot_row == row + rank_row.astype(jnp.int32)).astype(F32).astype(BF16)
        placing.append(place)
        placing_t.append(place_t)
        codes = dot(codes8, place)
        codes = jnp.sum(jnp.where(tile_rows == t, codes, 0.0), axis=0, keepdims=True)
        codes = jnp.broadcast_to(codes, (8, 2 * CELLS))
        code_halves[0].append(codes[:, :CELLS])
        code_halves[1].append(codes[:, CELLS:])
    code_rows = tile_major(jnp.concatenate(code_halves[0] + code_halves[1], axis=0))

    pl.semaphore_wait(barrier, REGIONS - 1 + MEMBERS - 1)
    halo(VECTORS[0], 0).start()
    halo(VECTORS[0], 1).start()
    send_columns(CODES, code_rows)

    def block_of(at, offset):
        inside = (at >= 0) & (at < REGIONS)
        entry = pattern_ref[jnp.clip(at, 0, REGIONS - 1), offset]
        entry = jnp.where(inside, entry, -1)
        total = jnp.zeros((CELLS, CELLS), F32)
        for k in range(KTYPES):
            total = total + table_ref[k].astype(F32) * (entry == k).astype(F32)
        return total.astype(BF16)

    for side in range(3):
        present = (region + side - 1 >= 0) & (region + side - 1 < REGIONS)
        keep = present.astype(F32)
        blocks[0, side] = (block_of(region, side).astype(F32) * keep).astype(BF16)
        back = block_of(region + side - 1, 2 - side)
        blocks[1, side] = dot_nt(identity, back).astype(BF16)
    zeros = jnp.zeros((LEV, LEV), BF16)
    vloc = vloc_ref[...]
    vloc_t = dot_nt(identity[:LEV, :LEV], vloc).astype(BF16)
    for i, v in enumerate((vloc, vloc_t)):
        vert[i] = jnp.concatenate(
            [jnp.concatenate([v, zeros], axis=1), jnp.concatenate([zeros, v], axis=1)], axis=0
        )

    loads[1].wait()
    loads[2].wait()
    for t in range(TILES):
        for i, part in enumerate(split(weight[t])):
            coupling[i, t] = dot(placing_t[t], dot(part, placing[t]).astype(BF16)).astype(BF16)
        high, low = split(innov[:, CELLS * t : CELLS * (t + 1)])
        innov_slots[t] = dot(high, placing[t]) + dot(low, placing[t])

    codes = get_columns(CODES)
    code_row = lax.broadcasted_iota(jnp.int32, (2 * CELLS, CELLS), 0)
    for z in range(16):
        want = codes[8 * z : 8 * z + 1, :].astype(jnp.int32) - 1
        onehot[:, CELLS * z : CELLS * (z + 1)] = (code_row == want).astype(F32).astype(BF16)
    loads[0].wait()

    def conv(which, n):
        return (
            dot(halo_in[n, 0], blocks[which, 0])
            + dot(halo_out[n], blocks[which, 1])
            + dot(halo_in[n, 1], blocks[which, 2])
        )

    def forward(it):
        n = VECTORS[it]
        wait_halo(n, 0)
        wait_halo(n, 1)
        spread = conv(0, n).astype(BF16)
        sums = [jnp.zeros((LEV, CELLS), F32) for _ in range(2)]
        for pair in range(OWN // 2):
            local = dot(vert[0], spread[128 * pair : 128 * (pair + 1)])
            for i in range(2):
                for s in range(2):
                    sums[s] = sums[s] + pert[2 * pair + i, s].astype(F32) * local[LEV * i : LEV * (i + 1)]
        n = SUMS[it]
        for to in range(MEMBERS):
            for s in range(2):
                part_out[n, to, LPM * s : LPM * (s + 1)] = sums[s][LPM * to : LPM * (to + 1)]
        part_in[n, member] = part_out[n, member]
        start_parts(n, False)
        parts_like(n).wait_recv()
        total = jnp.sum(part_in[n], axis=0)
        increment = jnp.concatenate([total[:LPM], total[LPM:]], axis=1).astype(BF16)
        sampled = dot(increment, onehot[...])
        send_columns(
            SAMPLES[it], jnp.concatenate([sampled[:, CELLS * z : CELLS * (z + 1)] for z in range(16)], axis=0)
        )

    def weighted(it):
        slots = tile_major(get_columns(SAMPLES[it]))
        departures, results = [], []
        for t in range(TILES):
            here = jnp.concatenate([slots[8 * t : 8 * t + 8], slots[64 + 8 * t : 72 + 8 * t]], axis=1)
            if it == 0:
                here = here - innov_slots[t]
                high, low = split(here)
                result = dot(high, coupling[0, t]) + dot(low, coupling[0, t]) + dot(high, coupling[1, t])
            else:
                high = here.astype(BF16)
                result = dot(high, coupling[0, t]) + dot(high, coupling[1, t])
            departures.append(here)
            results.append(result)
        return departures, results

    def backward(it, results):
        back = jnp.concatenate([x[:, :CELLS] for x in results] + [x[:, CELLS:] for x in results], axis=0)
        send_columns(RETURNS[it], tile_major(back))
        here = get_columns(RETURNS[it]).astype(BF16)
        here = jnp.concatenate([here[8 * z : 8 * z + 8] for z in range(16)], axis=1)
        adjoint = dot_nt(here, onehot[...])
        n = ADJOINTS[it]
        mine = jnp.concatenate([adjoint[:, :CELLS], adjoint[:, CELLS:]], axis=0)
        part_out[n, member] = mine
        part_in[n, member] = mine
        start_parts(n, True)
        parts_like(n).wait_recv()
        fields = part_in[n]
        fields = [fields[:, LPM * s : LPM * (s + 1)].reshape(LEV, CELLS) for s in range(2)]
        n = LIFTED[it]
        for pair in range(OWN // 2):
            projected = jnp.concatenate(
                [
                    pert[k, 0].astype(F32) * fields[0] + pert[k, 1].astype(F32) * fields[1]
                    for k in (2 * pair, 2 * pair + 1)
                ],
                axis=0,
            ).astype(BF16)
            halo_out[n, 128 * pair : 128 * (pair + 1)] = dot(vert[1], projected).astype(BF16)
        halo(n, 0).start()
        halo(n, 1).start()
        wait_halo(n, 0)
        wait_halo(n, 1)
        return conv(1, n)

    forward(0)
    _, results = weighted(0)
    first = -(control_ref[...] + backward(0, results))
    r0[...] = first
    halo_out[VECTORS[1]] = first.astype(BF16)
    halo(VECTORS[1], 0).start()
    halo(VECTORS[1], 1).start()

    forward(1)
    _, results = weighted(1)
    second = r0[...] + backward(1, results)
    q[...] = second
    halo_out[VECTORS[2]] = second.astype(BF16)
    halo(VECTORS[2], 0).start()
    halo(VECTORS[2], 1).start()

    forward(2)
    departures, results = weighted(2)
    curve = sum(jnp.sum(d * w, axis=0, keepdims=True) for d, w in zip(departures, results, strict=True))
    curve = curve[:, :CELLS] + curve[:, CELLS:]
    first, second = r0[...], q[...]
    rows = [
        jnp.sum(first * first, axis=0, keepdims=True),
        jnp.sum(first * second, axis=0, keepdims=True),
        jnp.sum(second * second, axis=0, keepdims=True),
        curve,
        jnp.zeros((12, CELLS), F32),
    ]
    mine = jnp.concatenate(rows, axis=0)
    n = MEMBER_SCALARS
    part_out[n, member] = mine
    part_in[n, member] = mine
    start_parts(n, True)
    parts_like(n).wait_recv()
    total = jnp.sum(part_in[n], axis=0)
    total = jnp.sum(total, axis=1, keepdims=True)
    lane = lax.broadcasted_iota(jnp.int32, (2, CELLS), 1)
    message = jnp.zeros((2, CELLS), F32)
    for i in range(4):
        message = jnp.where(lane == i, total[i : i + 1, :], message)
    for i in range(REGIONS):
        cols_out[SCALARS, i] = message
    cols_in[SCALARS, region] = message
    start_columns(SCALARS)
    columns_like(SCALARS).wait_recv()
    sums = jnp.sum(cols_in[SCALARS], axis=0)[0:1]
    lane = lane[0:1]
    norm, cross, square, bent = (
        jnp.sum(jnp.where(lane == i, sums, 0.0), axis=1, keepdims=True) for i in range(4)
    )
    step = norm / cross
    norm_next = norm - 2.0 * step * cross + step * step * square
    ratio = norm_next / norm
    along = 1.0 + ratio
    image = along * along * cross - 2.0 * along * step * square + step * step * (square + bent)
    step_next = norm_next / image
    out_ref[...] = control_ref[...] + (step + step_next * along) * first - (step_next * step) * second

    for n in range(7):
        columns_like(n).wait_send()
    for n in range(6):
        parts_like(n).wait_send()
    for n in range(5):
        for side in range(2):
            halo(n, side).wait_send()


def local(
    perturbations, control, vertical_loc, block_kernels, loc_pattern, obs_region, obs_slot, obs_cell, innovations,
    obs_weight,
):
    codes = (obs_slot * CELLS + obs_cell + 1).reshape(TILES, CELLS)
    vmem, smem, anywhere = (pl.BlockSpec(memory_space=s) for s in (pltpu.VMEM, pltpu.SMEM, pl.ANY))
    dma = pltpu.SemaphoreType.DMA
    out = pl.pallas_call(
        kernel,
        out_shape=jax.ShapeDtypeStruct((ROWS, CELLS), F32),
        in_specs=[anywhere, vmem, vmem, vmem, smem, vmem, vmem, anywhere, anywhere],
        out_specs=vmem,
        scratch_shapes=[
            pltpu.VMEM((OWN, 2, LEV, CELLS), BF16),
            pltpu.VMEM((TILES, CELLS, CELLS), F32),
            pltpu.VMEM((LPM, TILES * CELLS), F32),
            pltpu.VMEM((ROWS, CELLS), F32),
            pltpu.VMEM((ROWS, CELLS), F32),
            pltpu.VMEM((5, ROWS, CELLS), BF16),
            pltpu.VMEM((5, 2, ROWS, CELLS), BF16),
            pltpu.VMEM((8, CELLS), F32),
            pltpu.VMEM((7, REGIONS, 2, CELLS), F32),
            pltpu.VMEM((7, REGIONS, 2, CELLS), F32),
            pltpu.VMEM((6, MEMBERS, 2 * LPM, CELLS), F32),
            pltpu.VMEM((6, MEMBERS, 2 * LPM, CELLS), F32),
            pltpu.VMEM((2 * CELLS, 16 * CELLS), BF16),
            pltpu.VMEM((2, TILES, 2 * CELLS, 2 * CELLS), BF16),
            pltpu.VMEM((TILES, LPM, 2 * CELLS), F32),
            pltpu.VMEM((2, 3, CELLS, CELLS), BF16),
            pltpu.VMEM((2, 2 * LEV, 2 * LEV), BF16),
            dma((3,)),
            pltpu.SemaphoreType.REGULAR,
            dma((7,)), dma((7,)),
            dma((6,)), dma((6,)),
            dma((5, 2)), dma((5, 2)),
        ],
        compiler_params=pltpu.CompilerParams(collective_id=0, has_side_effects=True, vmem_limit_bytes=40 << 20),
    )(
        perturbations, control.reshape(ROWS, CELLS), vertical_loc, block_kernels, loc_pattern,
        obs_region.reshape(TILES, CELLS), codes, innovations, obs_weight,
    )
    return out.reshape(OWN, LEV, CELLS)


def solution(mesh):
    placed = (
        P("member", None, None, "region"),
        P("member", None, "region"),
        P(),
        P(),
        P(),
        P("region", None),
        P("region"),
        P("region"),
        P(None, "region"),
        P("region", None, None),
    )
    return jax.shard_map(
        local, mesh=mesh, in_specs=placed, out_specs=P("member", None, "region"), check_vma=False
    )
```

```python
import jax
import jax.numpy as jnp
from jax import lax
from jax.experimental import pallas as pl
from jax.experimental.pallas import tpu as pltpu
from jax.sharding import PartitionSpec as P

REGIONS, MEMBERS = 64, 8
OWN = 10
LEV, CELLS = 64, 128
ROWS = OWN * LEV
TILES = 8
LPM = LEV // MEMBERS
KTYPES = 4
CHUNKS = OWN // 2
CHUNK = ROWS // CHUNKS
EARLY = 2
F32, BF16 = jnp.float32, jnp.bfloat16
MESH = pl.DeviceIdType.MESH
CODES, SAMPLES, RETURNS, SCALARS = 0, (1, 3, 5), (2, 4), 6
SUMS, ADJOINTS, MEMBER_SCALARS = (0, 2, 4), (1, 3), 5
VECTORS, LIFTED = (0, 2, 4), (1, 3)


def dot(a, b):
    return jnp.dot(a, b, preferred_element_type=F32)


def dot_nt(a, b):
    return lax.dot_general(a, b, (((1,), (1,)), ((), ())), preferred_element_type=F32)


def bit_of(shape, axis, stride):
    return (lax.broadcasted_iota(jnp.int32, shape, axis) & stride) != 0


def swap_bits(x, row_stride, lane_stride):
    n = x.shape[0]
    row, lane = bit_of(x.shape, 0, row_stride), bit_of(x.shape, 1, lane_stride)
    up = pltpu.roll(pltpu.roll(x, n - row_stride, 0), lane_stride, 1)
    down = pltpu.roll(pltpu.roll(x, row_stride, 0), CELLS - lane_stride, 1)
    return jnp.where(row == lane, x, jnp.where(row, down, up))


def region_major(x):
    return swap_bits(swap_bits(x, 2, 32), 4, 64)


def tile_major(x):
    return swap_bits(swap_bits(swap_bits(x, 8, 4), 16, 8), 32, 16)


def split(x):
    high = x.astype(BF16)
    return high, (x - high.astype(F32)).astype(BF16)


def kernel(
    pert_hbm, control_hbm, vloc_hbm, table_hbm, pattern_hbm, region_hbm, slot_hbm, cell_hbm, innov_hbm, weight_hbm,
    out_ref,
    pert, control, vloc_ref, table, pattern, obs, weight, innov, r0, q, halo_out, halo_in,
    cols_out, cols_in, sums_out, sums_in, part_out, part_in,
    placing, onehot, coupling, innov_slots, blocks, vert,
    load_sem, col_send, col_recv, part_send, part_recv, halo_send, halo_recv,
):
    region, member = lax.axis_index("region"), lax.axis_index("member")
    left, right = lax.rem(region + (REGIONS - 1), REGIONS), lax.rem(region + 1, REGIONS)

    here = pl.multiple_of(member * LPM, LPM)
    pairs = [
        (region_hbm, obs.at[0]),
        (slot_hbm, obs.at[1]),
        (cell_hbm, obs.at[2]),
        (control_hbm, control),
        (table_hbm, table),
        (vloc_hbm, vloc_ref),
        (weight_hbm, weight),
        (innov_hbm.at[pl.ds(here, LPM)], innov),
        (pert_hbm, pert),
        (pattern_hbm, pattern),
    ]
    loads = [pltpu.make_async_copy(a, b, load_sem.at[i]) for i, (a, b) in enumerate(pairs)]
    barrier = pltpu.get_barrier_semaphore()

    def greet(i):
        pl.semaphore_signal(
            barrier, inc=1, device_id={"region": lax.rem(region + i, REGIONS)}, device_id_type=MESH
        )

    def greet_pair(i, _):
        greet(32 - i)
        greet(32 + i)
        return 0

    greet(32)
    lax.fori_loop(1, 32, greet_pair, 0)

    def greet_member(i, _):
        pl.semaphore_signal(
            barrier, inc=1, device_id={"member": lax.rem(member + i, MEMBERS)}, device_id_type=MESH
        )
        return 0

    lax.fori_loop(1, MEMBERS, greet_member, 0)
    for load in loads:
        load.start()

    def buffers(n):
        return (sums_out, sums_in) if n == SCALARS else (cols_out.at[n], cols_in.at[n])

    def start_columns(n):
        source, target = buffers(n)

        def one(i):
            to = lax.rem(region + i, REGIONS)
            pltpu.make_async_remote_copy(
                src_ref=source.at[to], dst_ref=target.at[region],
                send_sem=col_send.at[n], recv_sem=col_recv.at[n],
                device_id={"region": to}, device_id_type=MESH,
            ).start()

        def pair(j, _):
            one(32 - j)
            one(32 + j)
            return 0

        one(32)
        lax.fori_loop(1, 32, pair, 0)

    def columns_like(n):
        source, target = buffers(n)
        return pltpu.make_async_remote_copy(
            src_ref=source.at[pl.ds(0, REGIONS - 1)], dst_ref=target.at[pl.ds(0, REGIONS - 1)],
            send_sem=col_send.at[n], recv_sem=col_recv.at[n],
            device_id={"region": right}, device_id_type=MESH,
        )

    def start_parts(n, same):
        def one(i, _):
            to = lax.rem(member + i, MEMBERS)
            pltpu.make_async_remote_copy(
                src_ref=part_out.at[n, member if same else to], dst_ref=part_in.at[n, member],
                send_sem=part_send.at[n], recv_sem=part_recv.at[n],
                device_id={"member": to}, device_id_type=MESH,
            ).start()
            return 0

        lax.fori_loop(1, MEMBERS, one, 0)

    def parts_like(n):
        return pltpu.make_async_remote_copy(
            src_ref=part_out.at[n, pl.ds(0, MEMBERS - 1)], dst_ref=part_in.at[n, pl.ds(0, MEMBERS - 1)],
            send_sem=part_send.at[n], recv_sem=part_recv.at[n],
            device_id={"member": lax.rem(member + 1, MEMBERS)}, device_id_type=MESH,
        )

    def halo(n, side, chunk):
        rows = pl.ds(CHUNK * chunk, CHUNK)
        return pltpu.make_async_remote_copy(
            src_ref=halo_out.at[n, rows], dst_ref=halo_in.at[n, 1 - side, rows],
            send_sem=halo_send.at[n, side, chunk], recv_sem=halo_recv.at[n, 1 - side, chunk],
            device_id={"region": left if side == 0 else right}, device_id_type=MESH,
        )

    def send_halo(n, chunk, x):
        halo_out[n, CHUNK * chunk : CHUNK * (chunk + 1)] = x
        for side in range(2):
            halo(n, side, chunk).start()

    def wait_halo(n, chunk):
        rows = pl.ds(CHUNK * chunk, CHUNK)
        for side in range(2):
            pltpu.make_async_remote_copy(
                src_ref=halo_out.at[n, rows], dst_ref=halo_in.at[n, side, rows],
                send_sem=halo_send.at[n, 1 - side, chunk], recv_sem=halo_recv.at[n, side, chunk],
                device_id={"region": left if side == 0 else right}, device_id_type=MESH,
            ).wait_recv()

    def send_columns(n, x):
        cols_out[n] = region_major(x).astype(BF16).reshape(REGIONS, 2, CELLS)
        cols_in[n, region] = cols_out[n, region]
        start_columns(n)

    def get_columns(n):
        columns_like(n).wait_recv()
        return region_major(cols_in[n].reshape(2 * REGIONS, CELLS).astype(F32))

    for load in loads[:3]:
        load.wait()
    regions8 = obs[0]
    codes8 = (obs[1] * CELLS + obs[2] + 1).astype(F32).astype(BF16)
    iota_row = lax.broadcasted_iota(jnp.int32, (CELLS, CELLS), 0)
    iota_lane = lax.broadcasted_iota(jnp.int32, (CELLS, CELLS), 1)
    identity = (iota_row == iota_lane).astype(F32).astype(BF16)
    zz, xx = regions8 >> 2, regions8 & 3
    base8 = 128 * (zz >> 3) + 32 * xx + 4 * (zz & 7)
    base_cols = dot_nt(identity, base8.astype(F32).astype(BF16)).astype(jnp.int32)
    slot_lane = lax.broadcasted_iota(jnp.int32, (CELLS, 2 * CELLS), 1)
    slot_row = lax.broadcasted_iota(jnp.int32, (2 * CELLS, CELLS), 0)
    tile_rows = lax.broadcasted_iota(jnp.int32, (8, 2 * CELLS), 0)
    code_halves = [[], []]
    for t in range(TILES):
        col, row = base_cols[:, t : t + 1], base8[t : t + 1, :]
        same = col == row
        rank = jnp.sum((same & (iota_lane < iota_row)).astype(F32), axis=1, keepdims=True)
        place = (slot_lane == col + rank.astype(jnp.int32)).astype(F32).astype(BF16)
        placing[t] = place
        codes = dot(codes8, place)
        codes = jnp.sum(jnp.where(tile_rows == t, codes, 0.0), axis=0, keepdims=True)
        codes = jnp.broadcast_to(codes, (8, 2 * CELLS))
        code_halves[0].append(codes[:, :CELLS])
        code_halves[1].append(codes[:, CELLS:])
    code_rows = tile_major(jnp.concatenate(code_halves[0] + code_halves[1], axis=0))
    loads[3].wait()

    pl.semaphore_wait(barrier, REGIONS - 1 + MEMBERS - 1)
    for chunk in range(CHUNKS):
        send_halo(VECTORS[0], chunk, control[CHUNK * chunk : CHUNK * (chunk + 1)].astype(BF16))
    send_columns(CODES, code_rows)

    loads[4].wait()
    loads[5].wait()
    loads[9].wait()

    block_lane = lax.broadcasted_iota(jnp.int32, (1, REGIONS), 1)

    def block_of(at, offset):
        found = jnp.where(block_lane == at, pattern[offset : offset + 1, :].astype(F32), 0.0)
        entry = jnp.sum(found, axis=1, keepdims=True)
        total = jnp.zeros((CELLS, CELLS), F32)
        for k in range(KTYPES):
            total = total + table[k].astype(F32) * (entry == k).astype(F32)
        return total * ((at >= 0) & (at < REGIONS)).astype(F32)

    for side in range(3):
        present = (region + side - 1 >= 0) & (region + side - 1 < REGIONS)
        blocks[0, side] = (block_of(region, side) * present.astype(F32)).astype(BF16)
        blocks[1, side] = dot_nt(identity, block_of(region + side - 1, 2 - side).astype(BF16)).astype(BF16)
    zeros = jnp.zeros((LEV, LEV), BF16)
    vloc = vloc_ref[...]
    vloc_t = dot_nt(identity[:LEV, :LEV], vloc).astype(BF16)
    for i, v in enumerate((vloc, vloc_t)):
        vert[i] = jnp.concatenate(
            [jnp.concatenate([v, zeros], axis=1), jnp.concatenate([zeros, v], axis=1)], axis=0
        )
    loads[8].wait()
    loads[6].wait()
    loads[7].wait()

    def couple(t):
        row = base8[t : t + 1, :]
        same = base_cols[:, t : t + 1] == row
        rank = jnp.sum((same & (iota_row < iota_lane)).astype(F32), axis=0, keepdims=True)
        place_t = (slot_row == row + rank.astype(jnp.int32)).astype(F32).astype(BF16)
        place = placing[t]
        for i, part in enumerate(split(weight[t])):
            coupling[i, t] = dot(place_t, dot(part, place).astype(BF16)).astype(BF16)
        high, low = split(innov[:, CELLS * t : CELLS * (t + 1)])
        innov_slots[t] = dot(high, place) + dot(low, place)

    def make_onehot():
        codes = get_columns(CODES)
        code_row = lax.broadcasted_iota(jnp.int32, (2 * CELLS, CELLS), 0)
        for z in range(16):
            want = codes[8 * z : 8 * z + 1, :].astype(jnp.int32) - 1
            onehot[:, CELLS * z : CELLS * (z + 1)] = (code_row == want).astype(F32).astype(BF16)

    def conv(which, n, chunk):
        rows = slice(CHUNK * chunk, CHUNK * (chunk + 1))
        return (
            dot(halo_in[n, 0, rows], blocks[which, 0])
            + dot(halo_out[n, rows], blocks[which, 1])
            + dot(halo_in[n, 1, rows], blocks[which, 2])
        )

    def forward(it):
        sums = [jnp.zeros((LEV, CELLS), F32) for _ in range(2)]
        for chunk in range(CHUNKS):
            wait_halo(VECTORS[it], chunk)
            local = dot(vert[0], conv(0, VECTORS[it], chunk).astype(BF16))
            for i in range(2):
                for s in range(2):
                    sums[s] = sums[s] + pert[2 * chunk + i, s].astype(F32) * local[LEV * i : LEV * (i + 1)]
        n = SUMS[it]
        for to in range(MEMBERS):
            for s in range(2):
                part_out[n, to, LPM * s : LPM * (s + 1)] = sums[s][LPM * to : LPM * (to + 1)]
        part_in[n, member] = part_out[n, member]
        start_parts(n, False)
        if it == 0:
            for t in range(EARLY):
                couple(t)
            make_onehot()
        parts_like(n).wait_recv()
        total = jnp.sum(part_in[n], axis=0)
        increment = jnp.concatenate([total[:LPM], total[LPM:]], axis=1).astype(BF16)
        sampled = dot(increment, onehot[...])
        send_columns(
            SAMPLES[it], jnp.concatenate([sampled[:, CELLS * z : CELLS * (z + 1)] for z in range(16)], axis=0)
        )
        if it == 0:
            for t in range(EARLY, TILES):
                couple(t)

    def weighted(it):
        slots = tile_major(get_columns(SAMPLES[it]))
        departures, results = [], []
        for t in range(TILES):
            here = jnp.concatenate([slots[8 * t : 8 * t + 8], slots[64 + 8 * t : 72 + 8 * t]], axis=1)
            if it == 0:
                here = here - innov_slots[t]
                high, low = split(here)
                result = dot(high, coupling[0, t]) + dot(low, coupling[0, t]) + dot(high, coupling[1, t])
            else:
                high = here.astype(BF16)
                result = dot(high, coupling[0, t]) + dot(high, coupling[1, t])
            departures.append(here)
            results.append(result)
        return departures, results

    def backward(it, results, update):
        back = jnp.concatenate([x[:, :CELLS] for x in results] + [x[:, CELLS:] for x in results], axis=0)
        send_columns(RETURNS[it], tile_major(back))
        here = get_columns(RETURNS[it]).astype(BF16)
        here = jnp.concatenate([here[8 * z : 8 * z + 8] for z in range(16)], axis=1)
        adjoint = dot_nt(here, onehot[...])
        n = ADJOINTS[it]
        mine = jnp.concatenate([adjoint[:, :CELLS], adjoint[:, CELLS:]], axis=0)
        part_out[n, member] = mine
        part_in[n, member] = mine
        start_parts(n, True)
        parts_like(n).wait_recv()
        fields = part_in[n]
        fields = [fields[:, LPM * s : LPM * (s + 1)].reshape(LEV, CELLS) for s in range(2)]
        for chunk in range(CHUNKS):
            projected = jnp.concatenate(
                [
                    pert[k, 0].astype(F32) * fields[0] + pert[k, 1].astype(F32) * fields[1]
                    for k in (2 * chunk, 2 * chunk + 1)
                ],
                axis=0,
            ).astype(BF16)
            send_halo(LIFTED[it], chunk, dot(vert[1], projected).astype(BF16))
        for chunk in range(CHUNKS):
            wait_halo(LIFTED[it], chunk)
            update(chunk, slice(CHUNK * chunk, CHUNK * (chunk + 1)), conv(1, LIFTED[it], chunk))

    def residual(chunk, rows, back):
        value = -(control[rows] + back)
        r0[rows] = value
        send_halo(VECTORS[1], chunk, value.astype(BF16))

    forward(0)
    _, results = weighted(0)
    backward(0, results, residual)

    def image_of(chunk, rows, back):
        value = r0[rows] + back
        q[rows] = value
        send_halo(VECTORS[2], chunk, value.astype(BF16))

    forward(1)
    _, results = weighted(1)
    backward(1, results, image_of)

    forward(2)
    departures, results = weighted(2)
    curve = sum(jnp.sum(d * w, axis=0, keepdims=True) for d, w in zip(departures, results, strict=True))
    curve = curve[:, :CELLS] + curve[:, CELLS:]
    first, second = r0[...], q[...]
    rows = [
        jnp.sum(first * first, axis=0, keepdims=True),
        jnp.sum(first * second, axis=0, keepdims=True),
        jnp.sum(second * second, axis=0, keepdims=True),
        curve,
        jnp.zeros((12, CELLS), F32),
    ]
    mine = jnp.concatenate(rows, axis=0)
    n = MEMBER_SCALARS
    part_out[n, member] = mine
    part_in[n, member] = mine
    start_parts(n, True)
    parts_like(n).wait_recv()
    total = jnp.sum(part_in[n], axis=0)
    total = jnp.sum(total, axis=1, keepdims=True)
    lane = lax.broadcasted_iota(jnp.int32, (1, CELLS), 1)
    message = jnp.zeros((1, CELLS), F32)
    for i in range(4):
        message = jnp.where(lane == i, total[i : i + 1, :], message)
    sums_out[...] = jnp.broadcast_to(message[None], (REGIONS, 1, CELLS))
    sums_in[region] = message
    start_columns(SCALARS)
    columns_like(SCALARS).wait_recv()
    sums = jnp.sum(sums_in[...], axis=0)
    norm, cross, square, bent = (
        jnp.sum(jnp.where(lane == i, sums, 0.0), axis=1, keepdims=True) for i in range(4)
    )
    step = norm / cross
    norm_next = norm - 2.0 * step * cross + step * step * square
    ratio = norm_next / norm
    along = 1.0 + ratio
    image = along * along * cross - 2.0 * along * step * square + step * step * (square + bent)
    step_next = norm_next / image
    out_ref[...] = control[...] + (step + step_next * along) * first - (step_next * step) * second

    for n in range(7):
        columns_like(n).wait_send()
    for n in range(6):
        parts_like(n).wait_send()
    for n in range(5):
        for side in range(2):
            for chunk in range(CHUNKS):
                halo(n, side, chunk).wait_send()


def local(
    perturbations, control, vertical_loc, block_kernels, loc_pattern, obs_region, obs_slot, obs_cell, innovations,
    obs_weight,
):
    vmem, hbm = (pl.BlockSpec(memory_space=s) for s in (pltpu.VMEM, pltpu.HBM))
    dma = pltpu.SemaphoreType.DMA
    out = pl.pallas_call(
        kernel,
        out_shape=jax.ShapeDtypeStruct((ROWS, CELLS), F32),
        in_specs=[hbm] * 10,
        out_specs=vmem,
        scratch_shapes=[
            pltpu.VMEM((OWN, 2, LEV, CELLS), BF16),
            pltpu.VMEM((ROWS, CELLS), F32),
            pltpu.VMEM((LEV, LEV), BF16),
            pltpu.VMEM((KTYPES, CELLS, CELLS), BF16),
            pltpu.VMEM((3, REGIONS), jnp.int32),
            pltpu.VMEM((3, TILES, CELLS), jnp.int32),
            pltpu.VMEM((TILES, CELLS, CELLS), F32),
            pltpu.VMEM((LPM, TILES * CELLS), F32),
            pltpu.VMEM((ROWS, CELLS), F32),
            pltpu.VMEM((ROWS, CELLS), F32),
            pltpu.VMEM((5, ROWS, CELLS), BF16),
            pltpu.VMEM((5, 2, ROWS, CELLS), BF16),
            pltpu.VMEM((6, REGIONS, 2, CELLS), BF16),
            pltpu.VMEM((6, REGIONS, 2, CELLS), BF16),
            pltpu.VMEM((REGIONS, 1, CELLS), F32),
            pltpu.VMEM((REGIONS, 1, CELLS), F32),
            pltpu.VMEM((6, MEMBERS, 2 * LPM, CELLS), F32),
            pltpu.VMEM((6, MEMBERS, 2 * LPM, CELLS), F32),
            pltpu.VMEM((TILES, CELLS, 2 * CELLS), BF16),
            pltpu.VMEM((2 * CELLS, 16 * CELLS), BF16),
            pltpu.VMEM((2, TILES, 2 * CELLS, 2 * CELLS), BF16),
            pltpu.VMEM((TILES, LPM, 2 * CELLS), F32),
            pltpu.VMEM((2, 3, CELLS, CELLS), BF16),
            pltpu.VMEM((2, 2 * LEV, 2 * LEV), BF16),
            dma((10,)),
            dma((7,)), dma((7,)),
            dma((6,)), dma((6,)),
            dma((5, 2, CHUNKS)), dma((5, 2, CHUNKS)),
        ],
        compiler_params=pltpu.CompilerParams(collective_id=0, has_side_effects=True, vmem_limit_bytes=60 << 20),
    )(
        perturbations, control.reshape(ROWS, CELLS), vertical_loc, block_kernels, loc_pattern.T,
        obs_region.reshape(TILES, CELLS), obs_slot.reshape(TILES, CELLS), obs_cell.reshape(TILES, CELLS),
        innovations, obs_weight,
    )
    return out.reshape(OWN, LEV, CELLS)


def solution(mesh):
    placed = (
        P("member", None, None, "region"),
        P("member", None, "region"),
        P(),
        P(),
        P(),
        P("region", None),
        P("region"),
        P("region"),
        P(None, "region"),
        P("region", None, None),
    )
    return jax.shard_map(
        local, mesh=mesh, in_specs=placed, out_specs=P("member", None, "region"), check_vma=False
    )
```

```python
import jax
import jax.numpy as jnp
from jax import lax
from jax.experimental import pallas as pl
from jax.experimental.pallas import tpu as pltpu
from jax.sharding import PartitionSpec as P

REGIONS, MEMBERS = 64, 8
OWN = 10
LEV, CELLS = 64, 128
ROWS = OWN * LEV
TILES = 8
LPM = LEV // MEMBERS
KTYPES = 4
CHUNKS = OWN // 2
CHUNK = ROWS // CHUNKS
EARLY = 2
F32, BF16 = jnp.float32, jnp.bfloat16
MESH = pl.DeviceIdType.MESH
CODES, SAMPLES, RETURNS, SCALARS = 0, (1, 3, 5), (2, 4), 6
SUMS, ADJOINTS, MEMBER_SCALARS = (0, 2, 4), (1, 3), 5
VECTORS, LIFTED = (0, 2, 4), (1, 3)


def dot(a, b):
    return jnp.dot(a, b, preferred_element_type=F32)


def dot_nt(a, b):
    return lax.dot_general(a, b, (((1,), (1,)), ((), ())), preferred_element_type=F32)


def bit_of(shape, axis, stride):
    return (lax.broadcasted_iota(jnp.int32, shape, axis) & stride) != 0


def swap_bits(x, row_stride, lane_stride):
    n = x.shape[0]
    row, lane = bit_of(x.shape, 0, row_stride), bit_of(x.shape, 1, lane_stride)
    up = pltpu.roll(pltpu.roll(x, n - row_stride, 0), lane_stride, 1)
    down = pltpu.roll(pltpu.roll(x, row_stride, 0), CELLS - lane_stride, 1)
    return jnp.where(row == lane, x, jnp.where(row, down, up))


def region_major(x):
    return swap_bits(swap_bits(x, 2, 32), 4, 64)


def tile_major(x):
    return swap_bits(swap_bits(swap_bits(x, 8, 4), 16, 8), 32, 16)


def split(x):
    high = x.astype(BF16)
    return high, (x - high.astype(F32)).astype(BF16)


def kernel(
    pert_hbm, control_hbm, vloc_hbm, table_hbm, pattern_hbm, region_hbm, slot_hbm, cell_hbm, innov_hbm, weight_hbm,
    out_ref,
    pert, control, vloc_ref, table, pattern, obs, weight, innov, r0, q, halo_out, halo_in,
    cols_out, cols_in, sums_out, sums_in, part_out, part_in,
    placing, onehot, onehot_t, coupling, innov_slots, blocks, vert,
    load_sem, col_send, col_recv, part_send, part_recv, halo_send, halo_recv,
):
    region, member = lax.axis_index("region"), lax.axis_index("member")
    left, right = lax.rem(region + (REGIONS - 1), REGIONS), lax.rem(region + 1, REGIONS)

    here = pl.multiple_of(member * LPM, LPM)
    pairs = [
        (region_hbm, obs.at[0]),
        (slot_hbm, obs.at[1]),
        (cell_hbm, obs.at[2]),
        (control_hbm, control),
        (table_hbm, table),
        (vloc_hbm, vloc_ref),
        (weight_hbm, weight),
        (innov_hbm.at[pl.ds(here, LPM)], innov),
        (pert_hbm, pert),
        (pattern_hbm, pattern),
    ]
    loads = [pltpu.make_async_copy(a, b, load_sem.at[i]) for i, (a, b) in enumerate(pairs)]
    barrier = pltpu.get_barrier_semaphore()

    def greet(i):
        pl.semaphore_signal(
            barrier, inc=1, device_id={"region": lax.rem(region + i, REGIONS)}, device_id_type=MESH
        )

    def greet_pair(i, _):
        greet(32 - i)
        greet(32 + i)
        return 0

    greet(32)
    lax.fori_loop(1, 32, greet_pair, 0)

    def greet_member(i, _):
        pl.semaphore_signal(
            barrier, inc=1, device_id={"member": lax.rem(member + i, MEMBERS)}, device_id_type=MESH
        )
        return 0

    lax.fori_loop(1, MEMBERS, greet_member, 0)
    for load in loads:
        load.start()

    def buffers(n):
        return (sums_out, sums_in) if n == SCALARS else (cols_out.at[n], cols_in.at[n])

    def start_columns(n):
        source, target = buffers(n)

        def one(i):
            to = lax.rem(region + i, REGIONS)
            pltpu.make_async_remote_copy(
                src_ref=source.at[to], dst_ref=target.at[region],
                send_sem=col_send.at[n], recv_sem=col_recv.at[n],
                device_id={"region": to}, device_id_type=MESH,
            ).start()

        def pair(j, _):
            one(32 - j)
            one(32 + j)
            return 0

        one(32)
        lax.fori_loop(1, 32, pair, 0)

    def columns_like(n):
        source, target = buffers(n)
        return pltpu.make_async_remote_copy(
            src_ref=source.at[pl.ds(0, REGIONS - 1)], dst_ref=target.at[pl.ds(0, REGIONS - 1)],
            send_sem=col_send.at[n], recv_sem=col_recv.at[n],
            device_id={"region": right}, device_id_type=MESH,
        )

    def start_parts(n, same):
        def one(i, _):
            to = lax.rem(member + i, MEMBERS)
            pltpu.make_async_remote_copy(
                src_ref=part_out.at[n, member if same else to], dst_ref=part_in.at[n, member],
                send_sem=part_send.at[n], recv_sem=part_recv.at[n],
                device_id={"member": to}, device_id_type=MESH,
            ).start()
            return 0

        lax.fori_loop(1, MEMBERS, one, 0)

    def parts_like(n):
        return pltpu.make_async_remote_copy(
            src_ref=part_out.at[n, pl.ds(0, MEMBERS - 1)], dst_ref=part_in.at[n, pl.ds(0, MEMBERS - 1)],
            send_sem=part_send.at[n], recv_sem=part_recv.at[n],
            device_id={"member": lax.rem(member + 1, MEMBERS)}, device_id_type=MESH,
        )

    def halo(n, side, chunk):
        rows = pl.ds(CHUNK * chunk, CHUNK)
        return pltpu.make_async_remote_copy(
            src_ref=halo_out.at[n, rows], dst_ref=halo_in.at[n, 1 - side, rows],
            send_sem=halo_send.at[n, side, chunk], recv_sem=halo_recv.at[n, 1 - side, chunk],
            device_id={"region": left if side == 0 else right}, device_id_type=MESH,
        )

    def send_halo(n, chunk, x):
        halo_out[n, CHUNK * chunk : CHUNK * (chunk + 1)] = x
        for side in range(2):
            halo(n, side, chunk).start()

    def wait_halo(n, chunk):
        rows = pl.ds(CHUNK * chunk, CHUNK)
        for side in range(2):
            pltpu.make_async_remote_copy(
                src_ref=halo_out.at[n, rows], dst_ref=halo_in.at[n, side, rows],
                send_sem=halo_send.at[n, 1 - side, chunk], recv_sem=halo_recv.at[n, side, chunk],
                device_id={"region": left if side == 0 else right}, device_id_type=MESH,
            ).wait_recv()

    def stage_columns(n, x):
        cols_out[n] = region_major(x).astype(BF16).reshape(REGIONS, 2, CELLS)
        cols_in[n, region] = cols_out[n, region]

    def send_columns(n, x):
        stage_columns(n, x)
        start_columns(n)

    def get_columns(n):
        columns_like(n).wait_recv()
        return region_major(cols_in[n].reshape(2 * REGIONS, CELLS).astype(F32))

    for load in loads[:3]:
        load.wait()
    regions8 = obs[0]
    codes8 = (obs[1] * CELLS + obs[2] + 1).astype(F32).astype(BF16)
    iota_row = lax.broadcasted_iota(jnp.int32, (CELLS, CELLS), 0)
    iota_lane = lax.broadcasted_iota(jnp.int32, (CELLS, CELLS), 1)
    identity = (iota_row == iota_lane).astype(F32).astype(BF16)
    zz, xx = regions8 >> 2, regions8 & 3
    base8 = 128 * (zz >> 3) + 32 * xx + 4 * (zz & 7)
    base_cols = dot_nt(identity, base8.astype(F32).astype(BF16)).astype(jnp.int32)
    slot_lane = lax.broadcasted_iota(jnp.int32, (CELLS, 2 * CELLS), 1)
    slot_row = lax.broadcasted_iota(jnp.int32, (2 * CELLS, CELLS), 0)
    tile_rows = lax.broadcasted_iota(jnp.int32, (8, 2 * CELLS), 0)
    code_halves = [[], []]
    for t in range(TILES):
        col, row = base_cols[:, t : t + 1], base8[t : t + 1, :]
        same = col == row
        rank = jnp.sum((same & (iota_lane < iota_row)).astype(F32), axis=1, keepdims=True)
        place = (slot_lane == col + rank.astype(jnp.int32)).astype(F32).astype(BF16)
        placing[t] = place
        codes = dot(codes8, place)
        codes = jnp.sum(jnp.where(tile_rows == t, codes, 0.0), axis=0, keepdims=True)
        codes = jnp.broadcast_to(codes, (8, 2 * CELLS))
        code_halves[0].append(codes[:, :CELLS])
        code_halves[1].append(codes[:, CELLS:])
    code_rows = tile_major(jnp.concatenate(code_halves[0] + code_halves[1], axis=0))
    stage_columns(CODES, code_rows)
    loads[3].wait()
    halo_out[VECTORS[0]] = control[...].astype(BF16)

    pl.semaphore_wait(barrier, REGIONS - 1 + MEMBERS - 1)
    for chunk in range(CHUNKS):
        for side in range(2):
            halo(VECTORS[0], side, chunk).start()
    start_columns(CODES)

    loads[4].wait()
    loads[5].wait()
    loads[9].wait()

    block_lane = lax.broadcasted_iota(jnp.int32, (1, REGIONS), 1)

    def block_of(at, offset):
        found = jnp.where(block_lane == at, pattern[offset : offset + 1, :].astype(F32), 0.0)
        entry = jnp.sum(found, axis=1, keepdims=True)
        total = jnp.zeros((CELLS, CELLS), F32)
        for k in range(KTYPES):
            total = total + table[k].astype(F32) * (entry == k).astype(F32)
        return total * ((at >= 0) & (at < REGIONS)).astype(F32)

    for side in range(3):
        present = (region + side - 1 >= 0) & (region + side - 1 < REGIONS)
        blocks[0, side] = (block_of(region, side) * present.astype(F32)).astype(BF16)
        blocks[1, side] = dot_nt(identity, block_of(region + side - 1, 2 - side).astype(BF16)).astype(BF16)
    zeros = jnp.zeros((LEV, LEV), BF16)
    vloc = vloc_ref[...]
    vloc_t = dot_nt(identity[:LEV, :LEV], vloc).astype(BF16)
    for i, v in enumerate((vloc, vloc_t)):
        vert[i] = jnp.concatenate(
            [jnp.concatenate([v, zeros], axis=1), jnp.concatenate([zeros, v], axis=1)], axis=0
        )
    loads[8].wait()
    loads[6].wait()
    loads[7].wait()

    def couple(t):
        row = base8[t : t + 1, :]
        same = base_cols[:, t : t + 1] == row
        rank = jnp.sum((same & (iota_row < iota_lane)).astype(F32), axis=0, keepdims=True)
        place_t = (slot_row == row + rank.astype(jnp.int32)).astype(F32).astype(BF16)
        place = placing[t]
        for i, part in enumerate(split(weight[t])):
            coupling[i, t] = dot(place_t, dot(part, place).astype(BF16)).astype(BF16)
        high, low = split(innov[:, CELLS * t : CELLS * (t + 1)])
        innov_slots[t] = dot(high, place) + dot(low, place)

    def make_onehot_t(codes):
        cols = dot_nt(identity, codes.reshape(16, 8, CELLS)[:, 0].astype(BF16)).astype(jnp.int32) - 1
        code_lane = lax.broadcasted_iota(jnp.int32, (CELLS, 2 * CELLS), 1)
        for z in range(16):
            hit = (code_lane == cols[:, z : z + 1]).astype(F32).astype(BF16)
            onehot_t[CELLS * z : CELLS * (z + 1)] = hit

    def make_onehot(codes):
        code_row = lax.broadcasted_iota(jnp.int32, (2 * CELLS, CELLS), 0)
        for z in range(16):
            want = codes[8 * z : 8 * z + 1, :].astype(jnp.int32) - 1
            onehot[:, CELLS * z : CELLS * (z + 1)] = (code_row == want).astype(F32).astype(BF16)

    def conv(which, n, chunk):
        rows = slice(CHUNK * chunk, CHUNK * (chunk + 1))
        return (
            dot(halo_in[n, 0, rows], blocks[which, 0])
            + dot(halo_out[n, rows], blocks[which, 1])
            + dot(halo_in[n, 1, rows], blocks[which, 2])
        )

    def forward(it):
        sums = [jnp.zeros((LEV, CELLS), F32) for _ in range(2)]
        for chunk in range(CHUNKS):
            wait_halo(VECTORS[it], chunk)
            local = dot(vert[0], conv(0, VECTORS[it], chunk).astype(BF16))
            for i in range(2):
                for s in range(2):
                    sums[s] = sums[s] + pert[2 * chunk + i, s].astype(F32) * local[LEV * i : LEV * (i + 1)]
        n = SUMS[it]
        for to in range(MEMBERS):
            for s in range(2):
                part_out[n, to, LPM * s : LPM * (s + 1)] = sums[s][LPM * to : LPM * (to + 1)]
        part_in[n, member] = part_out[n, member]
        start_parts(n, False)
        if it == 0:
            for t in range(EARLY):
                couple(t)
            codes = get_columns(CODES)
            make_onehot(codes)
        parts_like(n).wait_recv()
        total = jnp.sum(part_in[n], axis=0)
        increment = jnp.concatenate([total[:LPM], total[LPM:]], axis=1).astype(BF16)
        sampled = dot(increment, onehot[...])
        send_columns(
            SAMPLES[it], jnp.concatenate([sampled[:, CELLS * z : CELLS * (z + 1)] for z in range(16)], axis=0)
        )
        if it == 0:
            for t in range(EARLY, TILES):
                couple(t)
            make_onehot_t(codes)

    def weighted(it):
        slots = tile_major(get_columns(SAMPLES[it]))
        departures, results = [], []
        for t in range(TILES):
            here = jnp.concatenate([slots[8 * t : 8 * t + 8], slots[64 + 8 * t : 72 + 8 * t]], axis=1)
            if it == 0:
                here = here - innov_slots[t]
                high, low = split(here)
                both = dot(jnp.concatenate([high, low], axis=0), coupling[0, t])
                result = both[:LPM] + both[LPM:] + dot(high, coupling[1, t])
            elif it == 1:
                high = here.astype(BF16)
                result = dot(high, coupling[0, t]) + dot(high, coupling[1, t])
            else:
                result = dot(here.astype(BF16), coupling[0, t])
            departures.append(here)
            results.append(result)
        return departures, results

    def backward(it, results, update):
        back = jnp.concatenate([x[:, :CELLS] for x in results] + [x[:, CELLS:] for x in results], axis=0)
        send_columns(RETURNS[it], tile_major(back))
        here = get_columns(RETURNS[it]).astype(BF16)
        here = jnp.concatenate([here[8 * z : 8 * z + 8] for z in range(16)], axis=1)
        adjoint = dot(here, onehot_t[...])
        n = ADJOINTS[it]
        mine = jnp.concatenate([adjoint[:, :CELLS], adjoint[:, CELLS:]], axis=0)
        part_out[n, member] = mine
        part_in[n, member] = mine
        start_parts(n, True)
        parts_like(n).wait_recv()
        fields = part_in[n]
        fields = [fields[:, LPM * s : LPM * (s + 1)].reshape(LEV, CELLS) for s in range(2)]
        for chunk in range(CHUNKS):
            projected = jnp.concatenate(
                [
                    pert[k, 0].astype(F32) * fields[0] + pert[k, 1].astype(F32) * fields[1]
                    for k in (2 * chunk, 2 * chunk + 1)
                ],
                axis=0,
            ).astype(BF16)
            send_halo(LIFTED[it], chunk, dot(vert[1], projected).astype(BF16))
        for chunk in range(CHUNKS):
            wait_halo(LIFTED[it], chunk)
            update(chunk, slice(CHUNK * chunk, CHUNK * (chunk + 1)), conv(1, LIFTED[it], chunk))

    def residual(chunk, rows, back):
        value = -(control[rows] + back)
        r0[rows] = value
        send_halo(VECTORS[1], chunk, value.astype(BF16))

    forward(0)
    _, results = weighted(0)
    backward(0, results, residual)

    def image_of(chunk, rows, back):
        value = r0[rows] + back
        q[rows] = value
        send_halo(VECTORS[2], chunk, value.astype(BF16))

    forward(1)
    _, results = weighted(1)
    backward(1, results, image_of)

    forward(2)
    departures, results = weighted(2)
    curve = sum(jnp.sum(d * w, axis=0, keepdims=True) for d, w in zip(departures, results, strict=True))
    curve = curve[:, :CELLS] + curve[:, CELLS:]
    first, second = r0[...], q[...]
    rows = [
        jnp.sum(first * first, axis=0, keepdims=True),
        jnp.sum(first * second, axis=0, keepdims=True),
        jnp.sum(second * second, axis=0, keepdims=True),
        curve,
        jnp.zeros((12, CELLS), F32),
    ]
    mine = jnp.concatenate(rows, axis=0)
    n = MEMBER_SCALARS
    part_out[n, member] = mine
    part_in[n, member] = mine
    start_parts(n, True)
    parts_like(n).wait_recv()
    total = jnp.sum(part_in[n], axis=0)
    total = jnp.sum(total, axis=1, keepdims=True)
    lane = lax.broadcasted_iota(jnp.int32, (1, CELLS), 1)
    message = jnp.zeros((1, CELLS), F32)
    for i in range(4):
        message = jnp.where(lane == i, total[i : i + 1, :], message)
    sums_out[...] = jnp.broadcast_to(message[None], (REGIONS, 1, CELLS))
    sums_in[region] = message
    start_columns(SCALARS)
    columns_like(SCALARS).wait_recv()
    sums = jnp.sum(sums_in[...], axis=0)
    norm, cross, square, bent = (
        jnp.sum(jnp.where(lane == i, sums, 0.0), axis=1, keepdims=True) for i in range(4)
    )
    step = norm / cross
    norm_next = norm - 2.0 * step * cross + step * step * square
    ratio = norm_next / norm
    along = 1.0 + ratio
    image = along * along * cross - 2.0 * along * step * square + step * step * (square + bent)
    step_next = norm_next / image
    out_ref[...] = control[...] + (step + step_next * along) * first - (step_next * step) * second

    for n in range(7):
        columns_like(n).wait_send()
    for n in range(6):
        parts_like(n).wait_send()
    for n in range(5):
        for side in range(2):
            for chunk in range(CHUNKS):
                halo(n, side, chunk).wait_send()


def local(
    perturbations, control, vertical_loc, block_kernels, loc_pattern, obs_region, obs_slot, obs_cell, innovations,
    obs_weight,
):
    vmem, hbm = (pl.BlockSpec(memory_space=s) for s in (pltpu.VMEM, pltpu.HBM))
    dma = pltpu.SemaphoreType.DMA
    out = pl.pallas_call(
        kernel,
        out_shape=jax.ShapeDtypeStruct((ROWS, CELLS), F32),
        in_specs=[hbm] * 10,
        out_specs=vmem,
        scratch_shapes=[
            pltpu.VMEM((OWN, 2, LEV, CELLS), BF16),
            pltpu.VMEM((ROWS, CELLS), F32),
            pltpu.VMEM((LEV, LEV), BF16),
            pltpu.VMEM((KTYPES, CELLS, CELLS), BF16),
            pltpu.VMEM((3, REGIONS), jnp.int32),
            pltpu.VMEM((3, TILES, CELLS), jnp.int32),
            pltpu.VMEM((TILES, CELLS, CELLS), F32),
            pltpu.VMEM((LPM, TILES * CELLS), F32),
            pltpu.VMEM((ROWS, CELLS), F32),
            pltpu.VMEM((ROWS, CELLS), F32),
            pltpu.VMEM((5, ROWS, CELLS), BF16),
            pltpu.VMEM((5, 2, ROWS, CELLS), BF16),
            pltpu.VMEM((6, REGIONS, 2, CELLS), BF16),
            pltpu.VMEM((6, REGIONS, 2, CELLS), BF16),
            pltpu.VMEM((REGIONS, 1, CELLS), F32),
            pltpu.VMEM((REGIONS, 1, CELLS), F32),
            pltpu.VMEM((6, MEMBERS, 2 * LPM, CELLS), F32),
            pltpu.VMEM((6, MEMBERS, 2 * LPM, CELLS), F32),
            pltpu.VMEM((TILES, CELLS, 2 * CELLS), BF16),
            pltpu.VMEM((2 * CELLS, 16 * CELLS), BF16),
            pltpu.VMEM((16 * CELLS, 2 * CELLS), BF16),
            pltpu.VMEM((2, TILES, 2 * CELLS, 2 * CELLS), BF16),
            pltpu.VMEM((TILES, LPM, 2 * CELLS), F32),
            pltpu.VMEM((2, 3, CELLS, CELLS), BF16),
            pltpu.VMEM((2, 2 * LEV, 2 * LEV), BF16),
            dma((10,)),
            dma((7,)), dma((7,)),
            dma((6,)), dma((6,)),
            dma((5, 2, CHUNKS)), dma((5, 2, CHUNKS)),
        ],
        compiler_params=pltpu.CompilerParams(collective_id=0, has_side_effects=True, vmem_limit_bytes=60 << 20),
    )(
        perturbations, control.reshape(ROWS, CELLS), vertical_loc, block_kernels, loc_pattern.T,
        obs_region.reshape(TILES, CELLS), obs_slot.reshape(TILES, CELLS), obs_cell.reshape(TILES, CELLS),
        innovations, obs_weight,
    )
    return out.reshape(OWN, LEV, CELLS)


def solution(mesh):
    placed = (
        P("member", None, None, "region"),
        P("member", None, "region"),
        P(),
        P(),
        P(),
        P("region", None),
        P("region"),
        P("region"),
        P(None, "region"),
        P("region", None, None),
    )
    return jax.shard_map(
        local, mesh=mesh, in_specs=placed, out_specs=P("member", None, "region"), check_vma=False
    )
```

```python
import jax
import jax.numpy as jnp
from jax import lax
from jax.experimental import pallas as pl
from jax.experimental.pallas import tpu as pltpu
from jax.sharding import PartitionSpec as P

REGIONS, MEMBERS = 64, 8
OWN = 10
LEV, CELLS = 64, 128
ROWS = OWN * LEV
TILES = 8
LPM = LEV // MEMBERS
KTYPES = 4
CHUNKS = OWN // 2
CHUNK = ROWS // CHUNKS
EARLY = 2
F32, BF16 = jnp.float32, jnp.bfloat16
MESH = pl.DeviceIdType.MESH
CODES, SAMPLES, RETURNS, SCALARS = 0, (1, 3, 5), (2, 4), 6
SUMS, ADJOINTS, MEMBER_SCALARS = (0, 2, 4), (1, 3), 5
VECTORS, LIFTED = (0, 2, 4), (1, 3)


def dot(a, b):
    return jnp.dot(a, b, preferred_element_type=F32)


def dot_nt(a, b):
    return lax.dot_general(a, b, (((1,), (1,)), ((), ())), preferred_element_type=F32)


def bit_of(shape, axis, stride):
    return (lax.broadcasted_iota(jnp.int32, shape, axis) & stride) != 0


def swap_bits(x, row_stride, lane_stride):
    n = x.shape[0]
    row, lane = bit_of(x.shape, 0, row_stride), bit_of(x.shape, 1, lane_stride)
    up = pltpu.roll(pltpu.roll(x, n - row_stride, 0), lane_stride, 1)
    down = pltpu.roll(pltpu.roll(x, row_stride, 0), CELLS - lane_stride, 1)
    return jnp.where(row == lane, x, jnp.where(row, down, up))


def region_major(x):
    return swap_bits(swap_bits(x, 2, 32), 4, 64)


def tile_major(x):
    return swap_bits(swap_bits(swap_bits(x, 8, 4), 16, 8), 32, 16)


def split(x):
    high = x.astype(BF16)
    return high, (x - high.astype(F32)).astype(BF16)


def kernel(
    pert_hbm, control_hbm, vloc_hbm, table_hbm, pattern_hbm, region_hbm, slot_hbm, cell_hbm, innov_hbm, weight_hbm,
    out_ref,
    pert, control, vloc_ref, table, pattern, obs, weight, innov, r0, q, own, halo_out, halo_in,
    cols_out, cols_in, sums_out, sums_in, part_out, part_in,
    placing, onehot, onehot_t, coupling, innov_slots, blocks, vert,
    load_sem, col_send, col_recv, part_send, part_recv, halo_send, halo_recv,
):
    region, member = lax.axis_index("region"), lax.axis_index("member")
    left, right = lax.rem(region + (REGIONS - 1), REGIONS), lax.rem(region + 1, REGIONS)

    here = pl.multiple_of(member * LPM, LPM)
    pairs = [
        (region_hbm, obs.at[0]),
        (slot_hbm, obs.at[1]),
        (cell_hbm, obs.at[2]),
        (control_hbm, control),
        (table_hbm, table),
        (vloc_hbm, vloc_ref),
        (weight_hbm, weight),
        (innov_hbm.at[pl.ds(here, LPM)], innov),
        (pert_hbm, pert),
        (pattern_hbm, pattern),
    ]
    loads = [pltpu.make_async_copy(a, b, load_sem.at[i]) for i, (a, b) in enumerate(pairs)]
    barrier = pltpu.get_barrier_semaphore()

    def greet(i):
        pl.semaphore_signal(
            barrier, inc=1, device_id={"region": lax.rem(region + i, REGIONS)}, device_id_type=MESH
        )

    def greet_pair(i, _):
        greet(32 - i)
        greet(32 + i)
        return 0

    greet(32)
    lax.fori_loop(1, 32, greet_pair, 0)

    def greet_member(i, _):
        pl.semaphore_signal(
            barrier, inc=1, device_id={"member": lax.rem(member + i, MEMBERS)}, device_id_type=MESH
        )
        return 0

    lax.fori_loop(1, MEMBERS, greet_member, 0)
    for load in loads:
        load.start()

    def buffers(n):
        return (sums_out, sums_in) if n == SCALARS else (cols_out.at[n], cols_in.at[n])

    def start_columns(n):
        source, target = buffers(n)

        def one(i):
            to = lax.rem(region + i, REGIONS)
            pltpu.make_async_remote_copy(
                src_ref=source.at[to], dst_ref=target.at[region],
                send_sem=col_send.at[n], recv_sem=col_recv.at[n],
                device_id={"region": to}, device_id_type=MESH,
            ).start()

        def pair(j, _):
            one(32 - j)
            one(32 + j)
            return 0

        one(32)
        lax.fori_loop(1, 32, pair, 0)

    def columns_like(n):
        source, target = buffers(n)
        return pltpu.make_async_remote_copy(
            src_ref=source.at[pl.ds(0, REGIONS - 1)], dst_ref=target.at[pl.ds(0, REGIONS - 1)],
            send_sem=col_send.at[n], recv_sem=col_recv.at[n],
            device_id={"region": right}, device_id_type=MESH,
        )

    def start_parts(n, same):
        def one(i, _):
            to = lax.rem(member + i, MEMBERS)
            pltpu.make_async_remote_copy(
                src_ref=part_out.at[n, member if same else to], dst_ref=part_in.at[n, member],
                send_sem=part_send.at[n], recv_sem=part_recv.at[n],
                device_id={"member": to}, device_id_type=MESH,
            ).start()
            return 0

        lax.fori_loop(1, MEMBERS, one, 0)

    def parts_like(n):
        return pltpu.make_async_remote_copy(
            src_ref=part_out.at[n, pl.ds(0, MEMBERS - 1)], dst_ref=part_in.at[n, pl.ds(0, MEMBERS - 1)],
            send_sem=part_send.at[n], recv_sem=part_recv.at[n],
            device_id={"member": lax.rem(member + 1, MEMBERS)}, device_id_type=MESH,
        )

    def halo(n, side, chunk):
        rows = pl.ds(CHUNK * chunk, CHUNK)
        return pltpu.make_async_remote_copy(
            src_ref=halo_out.at[n, rows], dst_ref=halo_in.at[n, 1 - side, rows],
            send_sem=halo_send.at[n, side, chunk], recv_sem=halo_recv.at[n, 1 - side, chunk],
            device_id={"region": left if side == 0 else right}, device_id_type=MESH,
        )

    def send_halo(n, chunk, x):
        halo_out[n, CHUNK * chunk : CHUNK * (chunk + 1)] = x
        for side in range(2):
            halo(n, side, chunk).start()

    def wait_halo(n, chunk):
        rows = pl.ds(CHUNK * chunk, CHUNK)
        for side in range(2):
            pltpu.make_async_remote_copy(
                src_ref=halo_out.at[n, rows], dst_ref=halo_in.at[n, side, rows],
                send_sem=halo_send.at[n, 1 - side, chunk], recv_sem=halo_recv.at[n, side, chunk],
                device_id={"region": left if side == 0 else right}, device_id_type=MESH,
            ).wait_recv()

    def stage_columns(n, x):
        cols_out[n] = region_major(x).astype(BF16).reshape(REGIONS, 2, CELLS)
        cols_in[n, region] = cols_out[n, region]

    def send_columns(n, x):
        stage_columns(n, x)
        start_columns(n)

    def get_columns(n):
        columns_like(n).wait_recv()
        return region_major(cols_in[n].reshape(2 * REGIONS, CELLS).astype(F32))

    for load in loads[:3]:
        load.wait()
    regions8 = obs[0]
    codes8 = (obs[1] * CELLS + obs[2] + 1).astype(F32).astype(BF16)
    iota_row = lax.broadcasted_iota(jnp.int32, (CELLS, CELLS), 0)
    iota_lane = lax.broadcasted_iota(jnp.int32, (CELLS, CELLS), 1)
    identity = (iota_row == iota_lane).astype(F32).astype(BF16)
    zz, xx = regions8 >> 2, regions8 & 3
    base8 = 128 * (zz >> 3) + 32 * xx + 4 * (zz & 7)
    base_cols = dot_nt(identity, base8.astype(F32).astype(BF16)).astype(jnp.int32)
    slot_lane = lax.broadcasted_iota(jnp.int32, (CELLS, 2 * CELLS), 1)
    slot_row = lax.broadcasted_iota(jnp.int32, (2 * CELLS, CELLS), 0)
    tile_rows = lax.broadcasted_iota(jnp.int32, (8, 2 * CELLS), 0)
    code_halves = [[], []]
    for t in range(TILES):
        col, row = base_cols[:, t : t + 1], base8[t : t + 1, :]
        same = col == row
        rank = jnp.sum((same & (iota_lane < iota_row)).astype(F32), axis=1, keepdims=True)
        place = (slot_lane == col + rank.astype(jnp.int32)).astype(F32).astype(BF16)
        placing[t] = place
        codes = dot(codes8, place)
        codes = jnp.sum(jnp.where(tile_rows == t, codes, 0.0), axis=0, keepdims=True)
        codes = jnp.broadcast_to(codes, (8, 2 * CELLS))
        code_halves[0].append(codes[:, :CELLS])
        code_halves[1].append(codes[:, CELLS:])
    code_rows = tile_major(jnp.concatenate(code_halves[0] + code_halves[1], axis=0))
    stage_columns(CODES, code_rows)
    loads[3].wait()
    halo_out[VECTORS[0]] = control[...].astype(BF16)

    pl.semaphore_wait(barrier, REGIONS - 1 + MEMBERS - 1)
    for chunk in range(CHUNKS):
        for side in range(2):
            halo(VECTORS[0], side, chunk).start()
    start_columns(CODES)

    loads[4].wait()
    loads[5].wait()
    loads[9].wait()

    block_lane = lax.broadcasted_iota(jnp.int32, (1, REGIONS), 1)

    def block_of(at, offset):
        found = jnp.where(block_lane == at, pattern[offset : offset + 1, :].astype(F32), 0.0)
        entry = jnp.sum(found, axis=1, keepdims=True)
        total = jnp.zeros((CELLS, CELLS), F32)
        for k in range(KTYPES):
            total = total + table[k].astype(F32) * (entry == k).astype(F32)
        return total * ((at >= 0) & (at < REGIONS)).astype(F32)

    for side in range(3):
        present = (region + side - 1 >= 0) & (region + side - 1 < REGIONS)
        blocks[0, side] = (block_of(region, side) * present.astype(F32)).astype(BF16)
        blocks[1, side] = dot_nt(identity, block_of(region + side - 1, 2 - side).astype(BF16)).astype(BF16)
    zeros = jnp.zeros((LEV, LEV), BF16)
    vloc = vloc_ref[...]
    vloc_t = dot_nt(identity[:LEV, :LEV], vloc).astype(BF16)
    for i, v in enumerate((vloc, vloc_t)):
        vert[i] = jnp.concatenate(
            [jnp.concatenate([v, zeros], axis=1), jnp.concatenate([zeros, v], axis=1)], axis=0
        )
    loads[8].wait()
    loads[6].wait()
    loads[7].wait()

    def couple(t):
        row = base8[t : t + 1, :]
        same = base_cols[:, t : t + 1] == row
        rank = jnp.sum((same & (iota_row < iota_lane)).astype(F32), axis=0, keepdims=True)
        place_t = (slot_row == row + rank.astype(jnp.int32)).astype(F32).astype(BF16)
        place = placing[t]
        for i, part in enumerate(split(weight[t])):
            coupling[i, t] = dot(place_t, dot(part, place).astype(BF16)).astype(BF16)
        high, low = split(innov[:, CELLS * t : CELLS * (t + 1)])
        innov_slots[t] = dot(high, place) + dot(low, place)

    def make_onehot_t(codes):
        cols = dot_nt(identity, codes.reshape(16, 8, CELLS)[:, 0].astype(BF16)).astype(jnp.int32) - 1
        code_lane = lax.broadcasted_iota(jnp.int32, (CELLS, 2 * CELLS), 1)
        for z in range(16):
            hit = (code_lane == cols[:, z : z + 1]).astype(F32).astype(BF16)
            onehot_t[CELLS * z : CELLS * (z + 1)] = hit

    def make_onehot(codes):
        code_row = lax.broadcasted_iota(jnp.int32, (2 * CELLS, CELLS), 0)
        for z in range(16):
            want = codes[8 * z : 8 * z + 1, :].astype(jnp.int32) - 1
            onehot[:, CELLS * z : CELLS * (z + 1)] = (code_row == want).astype(F32).astype(BF16)

    def own_block(which, n):
        own[...] = dot(halo_out[n], blocks[which, 1])

    def conv(which, n, chunk):
        rows = slice(CHUNK * chunk, CHUNK * (chunk + 1))
        return (
            dot(halo_in[n, 0, rows], blocks[which, 0])
            + own[rows]
            + dot(halo_in[n, 1, rows], blocks[which, 2])
        )

    def forward(it):
        own_block(0, VECTORS[it])
        sums = [jnp.zeros((LEV, CELLS), F32) for _ in range(2)]
        for chunk in range(CHUNKS):
            wait_halo(VECTORS[it], chunk)
            local = dot(vert[0], conv(0, VECTORS[it], chunk).astype(BF16))
            for i in range(2):
                for s in range(2):
                    sums[s] = sums[s] + pert[2 * chunk + i, s].astype(F32) * local[LEV * i : LEV * (i + 1)]
        n = SUMS[it]
        for to in range(MEMBERS):
            for s in range(2):
                part_out[n, to, LPM * s : LPM * (s + 1)] = sums[s][LPM * to : LPM * (to + 1)]
        part_in[n, member] = part_out[n, member]
        start_parts(n, False)
        if it == 0:
            for t in range(EARLY):
                couple(t)
            codes = get_columns(CODES)
            make_onehot(codes)
        parts_like(n).wait_recv()
        total = jnp.sum(part_in[n], axis=0)
        increment = jnp.concatenate([total[:LPM], total[LPM:]], axis=1).astype(BF16)
        sampled = dot(increment, onehot[...])
        send_columns(
            SAMPLES[it], jnp.concatenate([sampled[:, CELLS * z : CELLS * (z + 1)] for z in range(16)], axis=0)
        )
        if it == 0:
            for t in range(EARLY, TILES):
                couple(t)
            make_onehot_t(codes)

    def weighted(it):
        slots = tile_major(get_columns(SAMPLES[it]))
        departures, results = [], []
        for t in range(TILES):
            here = jnp.concatenate([slots[8 * t : 8 * t + 8], slots[64 + 8 * t : 72 + 8 * t]], axis=1)
            if it == 0:
                here = here - innov_slots[t]
                high, low = split(here)
                both = dot(jnp.concatenate([high, low], axis=0), coupling[0, t])
                result = both[:LPM] + both[LPM:] + dot(high, coupling[1, t])
            elif it == 1:
                high = here.astype(BF16)
                result = dot(high, coupling[0, t]) + dot(high, coupling[1, t])
            else:
                result = dot(here.astype(BF16), coupling[0, t])
            departures.append(here)
            results.append(result)
        return departures, results

    def backward(it, results, update):
        back = jnp.concatenate([x[:, :CELLS] for x in results] + [x[:, CELLS:] for x in results], axis=0)
        send_columns(RETURNS[it], tile_major(back))
        here = get_columns(RETURNS[it]).astype(BF16)
        here = jnp.concatenate([here[8 * z : 8 * z + 8] for z in range(16)], axis=1)
        adjoint = dot(here, onehot_t[...])
        n = ADJOINTS[it]
        mine = jnp.concatenate([adjoint[:, :CELLS], adjoint[:, CELLS:]], axis=0)
        part_out[n, member] = mine
        part_in[n, member] = mine
        start_parts(n, True)
        parts_like(n).wait_recv()
        fields = part_in[n]
        fields = [fields[:, LPM * s : LPM * (s + 1)].reshape(LEV, CELLS) for s in range(2)]
        for chunk in range(CHUNKS):
            projected = jnp.concatenate(
                [
                    pert[k, 0].astype(F32) * fields[0] + pert[k, 1].astype(F32) * fields[1]
                    for k in (2 * chunk, 2 * chunk + 1)
                ],
                axis=0,
            ).astype(BF16)
            send_halo(LIFTED[it], chunk, dot(vert[1], projected).astype(BF16))
        own_block(1, LIFTED[it])
        for chunk in range(CHUNKS):
            wait_halo(LIFTED[it], chunk)
            update(chunk, slice(CHUNK * chunk, CHUNK * (chunk + 1)), conv(1, LIFTED[it], chunk))

    def residual(chunk, rows, back):
        value = -(control[rows] + back)
        r0[rows] = value
        send_halo(VECTORS[1], chunk, value.astype(BF16))

    forward(0)
    _, results = weighted(0)
    backward(0, results, residual)

    def image_of(chunk, rows, back):
        value = r0[rows] + back
        q[rows] = value
        send_halo(VECTORS[2], chunk, value.astype(BF16))

    forward(1)
    _, results = weighted(1)
    backward(1, results, image_of)

    forward(2)
    departures, results = weighted(2)
    curve = sum(jnp.sum(d * w, axis=0, keepdims=True) for d, w in zip(departures, results, strict=True))
    curve = curve[:, :CELLS] + curve[:, CELLS:]
    first, second = r0[...], q[...]
    rows = [
        jnp.sum(first * first, axis=0, keepdims=True),
        jnp.sum(first * second, axis=0, keepdims=True),
        jnp.sum(second * second, axis=0, keepdims=True),
        curve,
        jnp.zeros((12, CELLS), F32),
    ]
    mine = jnp.concatenate(rows, axis=0)
    n = MEMBER_SCALARS
    part_out[n, member] = mine
    part_in[n, member] = mine
    start_parts(n, True)
    parts_like(n).wait_recv()
    total = jnp.sum(part_in[n], axis=0)
    total = jnp.sum(total, axis=1, keepdims=True)
    lane = lax.broadcasted_iota(jnp.int32, (1, CELLS), 1)
    message = jnp.zeros((1, CELLS), F32)
    for i in range(4):
        message = jnp.where(lane == i, total[i : i + 1, :], message)
    sums_out[...] = jnp.broadcast_to(message[None], (REGIONS, 1, CELLS))
    sums_in[region] = message
    start_columns(SCALARS)
    columns_like(SCALARS).wait_recv()
    sums = jnp.sum(sums_in[...], axis=0)
    norm, cross, square, bent = (
        jnp.sum(jnp.where(lane == i, sums, 0.0), axis=1, keepdims=True) for i in range(4)
    )
    step = norm / cross
    norm_next = norm - 2.0 * step * cross + step * step * square
    ratio = norm_next / norm
    along = 1.0 + ratio
    image = along * along * cross - 2.0 * along * step * square + step * step * (square + bent)
    step_next = norm_next / image
    out_ref[...] = control[...] + (step + step_next * along) * first - (step_next * step) * second

    for n in range(7):
        columns_like(n).wait_send()
    for n in range(6):
        parts_like(n).wait_send()
    for n in range(5):
        for side in range(2):
            for chunk in range(CHUNKS):
                halo(n, side, chunk).wait_send()


def local(
    perturbations, control, vertical_loc, block_kernels, loc_pattern, obs_region, obs_slot, obs_cell, innovations,
    obs_weight,
):
    vmem, hbm = (pl.BlockSpec(memory_space=s) for s in (pltpu.VMEM, pltpu.HBM))
    dma = pltpu.SemaphoreType.DMA
    out = pl.pallas_call(
        kernel,
        out_shape=jax.ShapeDtypeStruct((ROWS, CELLS), F32),
        in_specs=[hbm] * 10,
        out_specs=vmem,
        scratch_shapes=[
            pltpu.VMEM((OWN, 2, LEV, CELLS), BF16),
            pltpu.VMEM((ROWS, CELLS), F32),
            pltpu.VMEM((LEV, LEV), BF16),
            pltpu.VMEM((KTYPES, CELLS, CELLS), BF16),
            pltpu.VMEM((3, REGIONS), jnp.int32),
            pltpu.VMEM((3, TILES, CELLS), jnp.int32),
            pltpu.VMEM((TILES, CELLS, CELLS), F32),
            pltpu.VMEM((LPM, TILES * CELLS), F32),
            pltpu.VMEM((ROWS, CELLS), F32),
            pltpu.VMEM((ROWS, CELLS), F32),
            pltpu.VMEM((ROWS, CELLS), F32),
            pltpu.VMEM((5, ROWS, CELLS), BF16),
            pltpu.VMEM((5, 2, ROWS, CELLS), BF16),
            pltpu.VMEM((6, REGIONS, 2, CELLS), BF16),
            pltpu.VMEM((6, REGIONS, 2, CELLS), BF16),
            pltpu.VMEM((REGIONS, 1, CELLS), F32),
            pltpu.VMEM((REGIONS, 1, CELLS), F32),
            pltpu.VMEM((6, MEMBERS, 2 * LPM, CELLS), F32),
            pltpu.VMEM((6, MEMBERS, 2 * LPM, CELLS), F32),
            pltpu.VMEM((TILES, CELLS, 2 * CELLS), BF16),
            pltpu.VMEM((2 * CELLS, 16 * CELLS), BF16),
            pltpu.VMEM((16 * CELLS, 2 * CELLS), BF16),
            pltpu.VMEM((2, TILES, 2 * CELLS, 2 * CELLS), BF16),
            pltpu.VMEM((TILES, LPM, 2 * CELLS), F32),
            pltpu.VMEM((2, 3, CELLS, CELLS), BF16),
            pltpu.VMEM((2, 2 * LEV, 2 * LEV), BF16),
            dma((10,)),
            dma((7,)), dma((7,)),
            dma((6,)), dma((6,)),
            dma((5, 2, CHUNKS)), dma((5, 2, CHUNKS)),
        ],
        compiler_params=pltpu.CompilerParams(collective_id=0, has_side_effects=True, vmem_limit_bytes=60 << 20),
    )(
        perturbations, control.reshape(ROWS, CELLS), vertical_loc, block_kernels, loc_pattern.T,
        obs_region.reshape(TILES, CELLS), obs_slot.reshape(TILES, CELLS), obs_cell.reshape(TILES, CELLS),
        innovations, obs_weight,
    )
    return out.reshape(OWN, LEV, CELLS)


def solution(mesh):
    placed = (
        P("member", None, None, "region"),
        P("member", None, "region"),
        P(),
        P(),
        P(),
        P("region", None),
        P("region"),
        P("region"),
        P(None, "region"),
        P("region", None, None),
    )
    return jax.shard_map(
        local, mesh=mesh, in_specs=placed, out_specs=P("member", None, "region"), check_vma=False
    )
```
